32 devices in a mesh: row: 4 (over x, core), col: 8 (over z, y).
Axes of the slice: x: 2, y: 2, z: 4, core: 2. Of those that a mesh axis runs over, the one named last changes fastest.
Arguments:
- trailing: float32 [24576, 24576], P('row', 'col'), may hold values from -6 to 6
- panel_first: float32 [24576, 256], P(('row', 'col')), may hold values from -0.0390625 to 0.0390625
- panel_second: float32 [24576, 256], P(('row', 'col')), may hold values from -0.0390625 to 0.0390625
- link_block: float32 [256, 256], replicated, may hold values from -0.375 to 0.375
- inverse_first: float32 [256, 256], replicated, may hold values from -6 to 6
- inverse_second: float32 [256, 256], replicated, may hold values from -6 to 6
- tile_struct: int32 [2, 192], replicated, may hold values 0 or 1
Outputs:
- panel_out_first: float32 [24576, 256], P(('row', 'col'))
- diag_out_first: float32 [256, 256], replicated
- panel_out_second: float32 [24576, 256], P(('row', 'col'))
- cross_out_second: float32 [256, 256], replicated
- diag_out_second: float32 [256, 256], replicated
The draws below stay inside these ranges and needn't reach their ends.
All inputs are finite; a program needn't handle non-finite values.
Results may differ from the reference program's by a relative error of at most 0.000071.
Values sent between devices are 32-bit elements; how exact they have to be, the bound alone decides.
No kernel may reach another device: no remote copies, remote signals or barrier semaphores. Data moves between devices by JAX's collectives and lax.ppermute only.
A program may use at most 192 MiB of HBM per device.

```python
import jax
import jax.numpy as jnp
from jax import lax

M = 24576
W = 256
TILE = 128
TILES = 192


def set_ends(result, stream_key, low, high):
    longest = result.shape.index(max(result.shape))
    spots = []
    for shift in (0, 1):
        where = [jax.random.randint(jax.random.fold_in(stream_key, axis), (), 0, length) for axis, length in enumerate(result.shape)]
        where[longest] = (where[longest] + shift) % result.shape[longest]
        spots.append(tuple(where))
    return result.at[spots[0]].set(low).at[spots[1]].set(high)


def with_spikes(values, own_key, source, target, shards_of, factor):
    def block_of(position):
        return (jnp.arange(values.shape[position]) // (values.shape[position] // shards_of)).reshape((-1,) + (1,) * (values.ndim - 1 - position))

    near = jax.random.permutation(own_key, shards_of)[block_of(target)]
    far = (block_of(target) + shards_of // 2) % shards_of
    return jnp.where((block_of(source) == near) | (block_of(source) == far), factor * values, values)


def levels(key, dims, cuts, smallest, largest):
    level, own = 1.0, jax.random.fold_in(key, 6)
    for position, blocks in cuts:
        steps = jnp.exp(jax.random.uniform(jax.random.fold_in(own, position), (blocks,), jnp.float32, smallest / len(cuts), largest / len(cuts)))
        level = level * jnp.repeat(steps, dims[position] // blocks).reshape([-1 if axis == position else 1 for axis in range(len(dims))])
    return level


def centred(key, dims, scale, limit, cuts=(), kind=jnp.bfloat16):
    loudness = levels(key, dims, cuts, -0.22, 0.18) if cuts else 1.0
    array = jax.random.normal(key, dims, jnp.float32) * scale * loudness
    return jnp.minimum(jnp.maximum(array, -limit), limit).astype(kind)


def noise_with(own_key, dims, width, bound, split, heavy, kind=jnp.bfloat16):
    values = width * jax.random.normal(own_key, dims, jnp.float32)
    if split:
        values = values * levels(own_key, dims, split, -0.22, 0.18)
    return jnp.clip(with_spikes(values, jax.random.fold_in(own_key, 3), *heavy), -bound, bound).astype(kind)


def setup_inputs(seed: int = 0) -> dict:
    splits = jax.random.split(jax.random.key(seed), 8)
    trailing = noise_with(splits[0], (M, M), 1.0, 6.0, ((0, 4), (1, 8)), (1, 0, 8, 2.0), jnp.float32)
    panel_first = centred(splits[1], (M, W), M ** -0.5, 0.0390625, ((0, 32),), jnp.float32)
    panel_second = centred(splits[2], (M, W), M ** -0.5, 0.0390625, ((0, 32),), jnp.float32)
    link_block = centred(splits[3], (W, W), W ** -0.5, 0.375, (), jnp.float32)
    inverse_first = centred(splits[4], (W, W), 1.0, 6.0, (), jnp.float32)
    inverse_second = centred(splits[5], (W, W), 1.0, 6.0, (), jnp.float32)
    tile_struct = set_ends((jax.random.randint(splits[6], (2, TILES), 0, 4) < 3).astype(jnp.int32), jax.random.fold_in(splits[6], 1), 0, 1)
    return {"trailing": trailing, "panel_first": panel_first, "panel_second": panel_second, "link_block": link_block, "inverse_first": inverse_first, "inverse_second": inverse_second, "tile_struct": tile_struct}


def matmul(left, right):
    return jnp.dot(left, right, precision=lax.Precision.HIGHEST, preferred_element_type=jnp.float32)


def reference(trailing, panel_first, panel_second, link_block, inverse_first, inverse_second, tile_struct):
    row_mask = jnp.repeat(tile_struct, TILE, axis=1).astype(jnp.float32)
    lead_first = panel_first * row_mask[0][:, None]
    lead_second = panel_second * row_mask[1][:, None]
    panel_out_first = -matmul(trailing, lead_first)
    diag_out_first = inverse_first - matmul(lead_first.T, panel_out_first)
    reach = matmul(trailing, lead_second)
    panel_out_second = -(matmul(panel_out_first, link_block) + reach)
    cross_out_second = -(matmul(diag_out_first, link_block) + matmul(panel_out_first.T, lead_second))
    diag_out_second = inverse_second - matmul(link_block.T, cross_out_second) - matmul(lead_second.T, panel_out_second)
    return panel_out_first, diag_out_first, panel_out_second, cross_out_second, diag_out_second
```

```python
import functools

import jax
import jax.numpy as jnp
from jax import lax
from jax.experimental import pallas as pl
from jax.experimental.pallas import tpu as pltpu
from jax.sharding import PartitionSpec as P

TILE = 128
LAG = 2
HOLD = 1
VMEM = 32 * 2**20
GROUPS = ((0,), (1,), (2,), (3,), (4,), (5,), (6,), (7,))


def matmul(left, right):
    return jnp.dot(left, right, precision=lax.Precision.HIGHEST, preferred_element_type=jnp.float32)


def inner(left, right):
    return lax.dot_general(
        left,
        right,
        (((0,), (0,)), ((), ())),
        precision=lax.Precision.HIGHEST,
        preferred_element_type=jnp.float32,
    )


def ring_column(n, place):
    return jnp.where(place < n // 2, 2 * place, 2 * (n - 1 - place) + 1)


def ring_perm(n, sign):
    order = list(range(0, n, 2)) + list(range(n - 1, 0, -2))
    return [(order[i], order[(i + sign) % n]) for i in range(n)]


def permute_all(value, table):
    return lax.ppermute(value, ("row", "col"), table)


def block_tables(n_row, n_col):
    def at(x, core, z, y):
        return (x * 2 + core) * n_col + z * 2 + y

    over_x, over_z, spread_a, spread_b, swap = [], [], [], [], []
    for x in range(2):
        for core in range(2):
            for z in range(4):
                for y in range(2):
                    here = at(x, core, z, y)
                    plane = (z + core) % 2
                    over_x.append((here, here if plane == x else at(1 - x, 1 - core, z, y)))
                    owner = x if (z + core) % 2 == x else 1 - x
                    own_core = core if owner == x else 1 - core
                    over_z.append((here, at(x, z // 2, 2 * owner + own_core, y)))
                    if core == y:
                        spread_a.append((here, at(1 - x, core, z, y)))
                        spread_b.append((here, here))
                    else:
                        spread_a.append((here, at(x, 1 - core, z, 1 - y)))
                        spread_b.append((here, at(1 - x, 1 - core, z, 1 - y)))
                    swap.append((here, at(x, 1 - core, z, y)))
    return over_x, over_z, spread_a, spread_b, swap


def block_order(row_index, col_index):
    x, core = row_index // 2, row_index % 2
    z, y = col_index // 2, col_index % 2
    even = (x + z) % 2
    order = []
    for block in range(4):
        z_low, who = block // 2, block % 2
        first = jnp.where(who == y, 1 - even, even)
        order.append(jnp.where(who == core, 0, 2) + jnp.where(first == z_low, 0, 1))
    return order


def after(value, *others):
    return lax.optimization_barrier((value, others))[0]


def gather_rows(lead, n_row, n_col, ahead):
    if (n_row, n_col) == (4, 8):
        over_x, over_z, spread_a, spread_b, swap = block_tables(n_row, n_col)
        moved = permute_all(after(lead, *ahead[:1]), over_x)
        held = permute_all(after(moved, *ahead[1:2]), over_z)
        ready = after(held, *ahead[2:])
        one, two = permute_all(ready, spread_a), permute_all(ready, spread_b)
        return (one, two), (moved, held, one, two)
    table = [(s, s % n_row * n_col + s // n_row) for s in range(n_row * n_col)]
    return (lax.all_gather(permute_all(lead, table), "row", axis=0, tiled=True),), ()


def split_rows(pieces, n_row, n_col):
    if (n_row, n_col) == (4, 8):
        swap = block_tables(n_row, n_col)[4]
        pieces = [*pieces, *(permute_all(piece, swap) for piece in pieces)]
    rows = jnp.concatenate(pieces, 0)
    high = lax.reduce_precision(rows, 8, 7)
    return jnp.concatenate([high, rows - high], 1).astype(jnp.bfloat16)


def product_kernel(width, parts, place_ref, a_ref, b_ref, up_ref, down_ref):
    side = pl.program_id(0)
    deep = a_ref.shape[1] // parts
    part = None
    for piece in range(parts):
        a = a_ref[:, piece * deep : (piece + 1) * deep]
        high = a.astype(jnp.bfloat16)
        low = (a - high.astype(jnp.float32)).astype(jnp.bfloat16)
        b = b_ref[pl.ds(pl.multiple_of(place_ref[1 + piece] * deep, deep), deep), :]
        term = jnp.dot(high, b[:, :width], preferred_element_type=jnp.float32)
        term += jnp.dot(high, b[:, width:], preferred_element_type=jnp.float32)
        term += jnp.dot(low, b[:, :width], preferred_element_type=jnp.float32)
        part = term if part is None else part + term

    @pl.when(side == 0)
    def _():
        up_ref[...] = part

    @pl.when(side == 1)
    def _():
        down_ref[...] = part


def products(trailing, split, place, n_col, steps):
    rows, cols = trailing.shape
    half = rows // n_col // 2
    width = split.shape[1] // 2
    count, first = len(steps), steps[0]

    def a_index(side, step, place_ref):
        back = 1 + first + step
        spot = jnp.where(side == 0, place_ref[0] - back + n_col, place_ref[0] + back) % n_col
        return ring_column(n_col, spot) * 2 + side, 0

    spec = pltpu.PrefetchScalarGridSpec(
        num_scalar_prefetch=1,
        grid=(2, count),
        in_specs=[
            pl.BlockSpec((half, cols), a_index),
            pl.BlockSpec((cols, 2 * width), lambda side, step, place_ref: (0, 0)),
        ],
        out_specs=[
            pl.BlockSpec(
                (half, width),
                lambda side, step, place_ref: (jnp.where(side == 0, step, count - 1), 0),
            ),
            pl.BlockSpec(
                (half, width),
                lambda side, step, place_ref: (jnp.where(side == 0, 0, step), 0),
            ),
        ],
    )
    shape = jax.ShapeDtypeStruct((count * half, width), jnp.float32)
    up, down = pl.pallas_call(
        functools.partial(product_kernel, width, place.shape[0] - 1),
        grid_spec=spec,
        out_shape=(shape, shape),
        compiler_params=pltpu.CompilerParams(
            dimension_semantics=("arbitrary",) * 2, vmem_limit_bytes=VMEM
        ),
        cost_estimate=pl.CostEstimate(
            flops=2 * 3 * 2 * count * half * cols * width,
            bytes_accessed=4 * 2 * count * half * cols,
            transcendentals=0,
        ),
    )(place, trailing, split)
    return {
        step: (up[i * half : (i + 1) * half], down[i * half : (i + 1) * half])
        for i, step in enumerate(steps)
    }


class Ring:
    def __init__(self, trailing, split, place, n_col):
        self.operands, self.n_col = (trailing, split, place), n_col
        self.made, self.sent, self.step = {}, (), 0

    def make(self, *others):
        trailing, split, place = self.operands
        groups = GROUPS if self.n_col == 8 else [(i,) for i in range(self.n_col)]
        for group in groups:
            if group[0] == self.step:
                place = after(place, *self.sent, *others)
                self.made.update(products(trailing, split, place, self.n_col, group))
        return self.made[self.step]

    def advance(self, *others):
        up, down = self.make()
        if self.step:
            came_up = lax.ppermute(self.sent[0], "col", ring_perm(self.n_col, 1))
            came_down = lax.ppermute(self.sent[1], "col", ring_perm(self.n_col, -1))
            if others:
                came_up, came_down = after(came_up, *others), after(came_down, *others)
            up, down = came_up + up, came_down + down
        self.sent, self.step = (up, down), self.step + 1


def scatter_total(value, n):
    rows, cols = value.shape
    parts = lax.all_to_all(value.reshape(n, rows // n, cols), ("row", "col"), 0, 0)
    return jnp.sum(parts, axis=0)


def spread_total(mine, n):
    spread = lax.all_to_all(jnp.broadcast_to(mine[None], (n,) + mine.shape), ("row", "col"), 0, 0)
    return spread.reshape(-1, mine.shape[1])


def on_device(
    trailing, panel_first, panel_second, link_block, inverse_first, inverse_second, tile_struct
):
    n_row, n_col = lax.axis_size("row"), lax.axis_size("col")
    n = n_row * n_col
    row_index, col_index = lax.axis_index("row"), lax.axis_index("col")
    count, width = panel_first.shape
    offset = (row_index * n_col + col_index) * count
    row_mask = jnp.repeat(tile_struct, TILE, axis=1)
    local_mask = lax.dynamic_slice_in_dim(row_mask, offset, count, 1).astype(jnp.float32)
    leads = (panel_first * local_mask[0][:, None], panel_second * local_mask[1][:, None])
    lead_first, lead_second = leads

    ring_place = jnp.where(col_index % 2 == 0, col_index // 2, n_col - (col_index + 1) // 2)
    if (n_row, n_col) == (4, 8):
        order = block_order(row_index, col_index)
    else:
        order = list(range(n_row))
    place = jnp.stack([jnp.asarray(v, jnp.int32) for v in [ring_place] + order])

    pieces_first, ahead = gather_rows(lead_first, n_row, n_col, ())
    pieces_second, _ = gather_rows(lead_second, n_row, n_col, ahead)
    first = Ring(trailing, split_rows(pieces_first, n_row, n_col), place, n_col)
    for _ in range(LAG):
        first.advance()
    pieces_second = [after(piece, *first.made[HOLD]) for piece in pieces_second]
    second = Ring(trailing, split_rows(pieces_second, n_row, n_col), place, n_col)
    for _ in range(LAG, n_col):
        second.advance()
        first.advance()
    panel_out_first = -jnp.concatenate(first.sent, 0)
    both = scatter_total(
        jnp.concatenate(
            [inner(lead_first, panel_out_first), inner(panel_out_first, lead_second)], 1
        ),
        n,
    )
    for _ in range(LAG - 1):
        second.advance()
    second.advance(both)
    reach = jnp.concatenate(second.sent, 0)
    panel_out_second = -(matmul(panel_out_first, link_block) + reach)
    both = spread_total(both, n)
    diag_sum, cross_sum = both[:, :width], both[:, width:]
    reach_sum = spread_total(scatter_total(inner(lead_second, reach), n), n)
    diag_out_first = inverse_first - diag_sum
    cross_out_second = -(matmul(diag_out_first, link_block) + cross_sum)
    diag_out_second = (
        inverse_second
        - inner(link_block, cross_out_second)
        + matmul(cross_sum.T, link_block)
        + reach_sum
    )
    return (panel_out_first, diag_out_first, panel_out_second, cross_out_second, diag_out_second)


def solution(mesh):
    return jax.shard_map(
        on_device,
        mesh=mesh,
        in_specs=(
            P("row", "col"),
            P(("row", "col"), None),
            P(("row", "col"), None),
            P(),
            P(),
            P(),
            P(),
        ),
        out_specs=(P(("row", "col"), None), P(), P(("row", "col"), None), P(), P()),
        check_vma=False,
    )
```

```python
import functools

import jax
import jax.numpy as jnp
from jax import lax
from jax.experimental import pallas as pl
from jax.experimental.pallas import tpu as pltpu
from jax.sharding import PartitionSpec as P

TILE = 128
VMEM = 48 * 2**20


def matmul(left, right):
    return jnp.dot(left, right, precision=lax.Precision.HIGHEST, preferred_element_type=jnp.float32)


def inner(left, right):
    return lax.dot_general(
        left,
        right,
        (((0,), (0,)), ((), ())),
        precision=lax.Precision.HIGHEST,
        preferred_element_type=jnp.float32,
    )


def ring_column(n, place):
    return jnp.where(place < n // 2, 2 * place, 2 * (n - 1 - place) + 1)


def ring_perm(n, sign):
    order = list(range(0, n, 2)) + list(range(n - 1, 0, -2))
    return [(order[i], order[(i + sign) % n]) for i in range(n)]


def permute_all(value, table):
    return lax.ppermute(value, ("row", "col"), table)


def block_tables(n_row, n_col):
    def at(x, core, z, y):
        return (x * 2 + core) * n_col + z * 2 + y

    over_x, over_z, spread_a, spread_b, swap = [], [], [], [], []
    for x in range(2):
        for core in range(2):
            for z in range(4):
                for y in range(2):
                    here = at(x, core, z, y)
                    plane = (z + core) % 2
                    over_x.append((here, here if plane == x else at(1 - x, 1 - core, z, y)))
                    owner = x if (z + core) % 2 == x else 1 - x
                    own_core = core if owner == x else 1 - core
                    over_z.append((here, at(x, z // 2, 2 * owner + own_core, y)))
                    if core == y:
                        spread_a.append((here, at(1 - x, core, z, y)))
                        spread_b.append((here, here))
                    else:
                        spread_a.append((here, at(x, 1 - core, z, 1 - y)))
                        spread_b.append((here, at(1 - x, 1 - core, z, 1 - y)))
                    swap.append((here, at(x, 1 - core, z, y)))
    return over_x, over_z, spread_a, spread_b, swap


def block_order(row_index, col_index):
    x, core = row_index // 2, row_index % 2
    z, y = col_index // 2, col_index % 2
    even = (x + z) % 2
    order = []
    for block in range(4):
        z_low, who = block // 2, block % 2
        first = jnp.where(who == y, 1 - even, even)
        order.append(jnp.where(who == core, 0, 2) + jnp.where(first == z_low, 0, 1))
    return order


def after(value, *others):
    return lax.optimization_barrier((value, others))[0]


def send_rows(lead, n_row, n_col, *ahead):
    if (n_row, n_col) == (4, 8):
        over_x, over_z = block_tables(n_row, n_col)[:2]
        moved = permute_all(after(lead, *ahead[:1]), over_x)
        return moved, permute_all(moved, over_z)
    table = [(s, s % n_row * n_col + s // n_row) for s in range(n_row * n_col)]
    return lead, permute_all(lead, table)


def spread_rows(rows, n_row, n_col):
    if (n_row, n_col) == (4, 8):
        spread_a, spread_b = block_tables(n_row, n_col)[2:4]
        return permute_all(rows, spread_a), permute_all(rows, spread_b)
    return (lax.all_gather(rows, "row", axis=0, tiled=True),)


def split_rows(pieces, n_row, n_col):
    if (n_row, n_col) == (4, 8):
        swap = block_tables(n_row, n_col)[4]
        pieces = [*pieces, *(permute_all(piece, swap) for piece in pieces)]
    rows = jnp.concatenate(pieces, 0)
    high = lax.reduce_precision(rows, 8, 7)
    return jnp.concatenate([high, rows - high], 1).astype(jnp.bfloat16)


def product_kernel(count, place_ref, a_ref, *refs):
    side = pl.program_id(0)
    b_refs, out_refs = refs[:count], refs[count:]
    parts = place_ref.shape[0] - 1
    deep = a_ref.shape[1] // parts
    width = b_refs[0].shape[1] // 2
    sums = [None] * count
    for piece in range(parts):
        a = a_ref[:, piece * deep : (piece + 1) * deep]
        high = a.astype(jnp.bfloat16)
        low = (a - high.astype(jnp.float32)).astype(jnp.bfloat16)
        rows = pl.ds(pl.multiple_of(place_ref[1 + piece] * deep, deep), deep)
        for i, b_ref in enumerate(b_refs):
            b = b_ref[rows, :]
            term = jnp.dot(high, b[:, :width], preferred_element_type=jnp.float32)
            term += jnp.dot(high, b[:, width:], preferred_element_type=jnp.float32)
            term += jnp.dot(low, b[:, :width], preferred_element_type=jnp.float32)
            sums[i] = term if sums[i] is None else sums[i] + term

    @pl.when(side == 0)
    def _():
        for i in range(count):
            out_refs[2 * i][...] = sums[i]

    @pl.when(side == 1)
    def _():
        for i in range(count):
            out_refs[2 * i + 1][...] = sums[i]


def products(trailing, splits, place, n_col, step):
    rows, cols = trailing.shape
    half = rows // n_col // 2
    width = splits[0].shape[1] // 2
    count = len(splits)

    def a_index(side, place_ref):
        back = 1 + step
        spot = jnp.where(side == 0, place_ref[0] - back + n_col, place_ref[0] + back) % n_col
        return ring_column(n_col, spot) * 2 + side, 0

    spec = pltpu.PrefetchScalarGridSpec(
        num_scalar_prefetch=1,
        grid=(2,),
        in_specs=[pl.BlockSpec((half, cols), a_index)]
        + [pl.BlockSpec((cols, 2 * width), lambda side, place_ref: (0, 0))] * count,
        out_specs=[pl.BlockSpec((half, width), lambda side, place_ref: (0, 0))] * (2 * count),
    )
    sums = pl.pallas_call(
        functools.partial(product_kernel, count),
        grid_spec=spec,
        out_shape=[jax.ShapeDtypeStruct((half, width), jnp.float32)] * (2 * count),
        compiler_params=pltpu.CompilerParams(
            dimension_semantics=("arbitrary",), vmem_limit_bytes=VMEM
        ),
        cost_estimate=pl.CostEstimate(
            flops=2 * 3 * 2 * half * cols * width * count,
            bytes_accessed=4 * 2 * half * cols,
            transcendentals=0,
        ),
    )(place, trailing, *splits)
    return [(sums[2 * i], sums[2 * i + 1]) for i in range(count)]


class Ring:
    def __init__(self, n_col):
        self.n_col, self.sent, self.step = n_col, (), 0

    def advance(self, made, *others):
        up, down = made
        if self.step:
            came_up = lax.ppermute(self.sent[0], "col", ring_perm(self.n_col, 1))
            came_down = lax.ppermute(self.sent[1], "col", ring_perm(self.n_col, -1))
            if others:
                came_up, came_down = after(came_up, *others), after(came_down, *others)
            up, down = came_up + up, came_down + down
        self.sent, self.step = (up, down), self.step + 1


def scatter_total(value, n, axes=("row", "col")):
    rows, cols = value.shape
    parts = lax.all_to_all(value.reshape(n, rows // n, cols), axes, 0, 0)
    return jnp.sum(parts, axis=0)


def spread_total(mine, n, axes=("row", "col")):
    spread = lax.all_to_all(jnp.broadcast_to(mine[None], (n,) + mine.shape), axes, 0, 0)
    return spread.reshape(-1, mine.shape[1])


def exchange_total(value):
    row_index = lax.axis_index("row")
    bits = [row_index % 2, row_index // 2]

    def partners(step):
        return [(i, i ^ step) for i in range(4)]

    for bit, step in zip(bits, (1, 2)):
        half = value.shape[0] // 2
        away = lax.dynamic_slice_in_dim(value, (1 - bit) * half, half, 0)
        kept = lax.dynamic_slice_in_dim(value, bit * half, half, 0)
        value = kept + lax.ppermute(away, "row", partners(step))
    value = spread_total(scatter_total(value, 8, "col"), 8, "col")
    for bit, step in ((bits[1], 2), (bits[0], 1)):
        other = lax.ppermute(value, "row", partners(step))
        value = jnp.where(
            bit == 0, jnp.concatenate([value, other], 0), jnp.concatenate([other, value], 0)
        )
    return value


def total(value, n_row, n_col):
    if (n_row, n_col) == (4, 8):
        return exchange_total(value)
    return spread_total(scatter_total(value, n_row * n_col), n_row * n_col)


def on_device(
    trailing, panel_first, panel_second, link_block, inverse_first, inverse_second, tile_struct
):
    n_row, n_col = lax.axis_size("row"), lax.axis_size("col")
    row_index, col_index = lax.axis_index("row"), lax.axis_index("col")
    count, width = panel_first.shape
    offset = (row_index * n_col + col_index) * count
    row_mask = jnp.repeat(tile_struct, TILE, axis=1)
    local_mask = lax.dynamic_slice_in_dim(row_mask, offset, count, 1).astype(jnp.float32)
    leads = (panel_first * local_mask[0][:, None], panel_second * local_mask[1][:, None])
    lead_first, lead_second = leads

    ring_place = jnp.where(col_index % 2 == 0, col_index // 2, n_col - (col_index + 1) // 2)
    if (n_row, n_col) == (4, 8):
        order = block_order(row_index, col_index)
    else:
        order = [0]
    place = jnp.stack([jnp.asarray(v, jnp.int32) for v in [ring_place] + order])

    splits = []
    for lead in leads:
        held = send_rows(lead, n_row, n_col)[1]
        splits.append(split_rows(spread_rows(held, n_row, n_col), n_row, n_col))
    first, second = Ring(n_col), Ring(n_col)
    for step in range(n_col):
        made = products(trailing, splits, after(place, *first.sent, *second.sent), n_col, step)
        first.advance(made[0])
        second.advance(made[1])
    panel_out_first = -jnp.concatenate(first.sent, 0)
    reach = jnp.concatenate(second.sent, 0)
    panel_out_second = -(matmul(panel_out_first, link_block) + reach)
    local = jnp.concatenate(
        [
            inner(lead_first, panel_out_first),
            inner(panel_out_first, lead_second),
            inner(lead_second, reach),
        ],
        1,
    )
    sums = total(local, n_row, n_col)
    diag_sum, cross_sum, reach_sum = (sums[:, i * width : (i + 1) * width] for i in range(3))
    diag_out_first = inverse_first - diag_sum
    cross_out_second = -(matmul(diag_out_first, link_block) + cross_sum)
    diag_out_second = (
        inverse_second
        - inner(link_block, cross_out_second)
        + matmul(cross_sum.T, link_block)
        + reach_sum
    )
    return (panel_out_first, diag_out_first, panel_out_second, cross_out_second, diag_out_second)


def solution(mesh):
    return jax.shard_map(
        on_device,
        mesh=mesh,
        in_specs=(
            P("row", "col"),
            P(("row", "col"), None),
            P(("row", "col"), None),
            P(),
            P(),
            P(),
            P(),
        ),
        out_specs=(P(("row", "col"), None), P(), P(("row", "col"), None), P(), P()),
        check_vma=False,
    )
```

```python
import functools

import jax
import jax.numpy as jnp
from jax import lax
from jax.experimental import pallas as pl
from jax.experimental.pallas import tpu as pltpu
from jax.sharding import PartitionSpec as P

TILE = 128
VMEM = 48 * 2**20


def matmul(left, right):
    return jnp.dot(left, right, precision=lax.Precision.HIGHEST, preferred_element_type=jnp.float32)


def inner(left, right):
    return lax.dot_general(
        left,
        right,
        (((0,), (0,)), ((), ())),
        precision=lax.Precision.HIGHEST,
        preferred_element_type=jnp.float32,
    )


def ring_column(n, place):
    return jnp.where(place < n // 2, 2 * place, 2 * (n - 1 - place) + 1)


def ring_perm(n, sign):
    order = list(range(0, n, 2)) + list(range(n - 1, 0, -2))
    return [(order[i], order[(i + sign) % n]) for i in range(n)]


def permute_all(value, table):
    return lax.ppermute(value, ("row", "col"), table)


def block_tables(n_row, n_col):
    def at(x, core, z, y):
        return (x * 2 + core) * n_col + z * 2 + y

    over_x, over_z, spread_a, spread_b, swap = [], [], [], [], []
    for x in range(2):
        for core in range(2):
            for z in range(4):
                for y in range(2):
                    here = at(x, core, z, y)
                    plane = (z + core) % 2
                    over_x.append((here, here if plane == x else at(1 - x, 1 - core, z, y)))
                    owner = x if (z + core) % 2 == x else 1 - x
                    own_core = core if owner == x else 1 - core
                    over_z.append((here, at(x, z // 2, 2 * owner + own_core, y)))
                    if core == y:
                        spread_a.append((here, at(1 - x, core, z, y)))
                        spread_b.append((here, here))
                    else:
                        spread_a.append((here, at(x, 1 - core, z, 1 - y)))
                        spread_b.append((here, at(1 - x, 1 - core, z, 1 - y)))
                    swap.append((here, at(x, 1 - core, z, y)))
    return over_x, over_z, spread_a, spread_b, swap


def block_order(row_index, col_index):
    x, core = row_index // 2, row_index % 2
    z, y = col_index // 2, col_index % 2
    even = (x + z) % 2
    order = []
    for who in (core, 1 - core):
        first = jnp.where(who == y, 1 - even, even)
        order += [first * 2 + who, (1 - first) * 2 + who]
    return order


def after(value, *others):
    return lax.optimization_barrier((value, others))[0]


def send_rows(lead, n_row, n_col, *ahead):
    if (n_row, n_col) == (4, 8):
        over_x, over_z = block_tables(n_row, n_col)[:2]
        moved = permute_all(after(lead, *ahead[:1]), over_x)
        return moved, permute_all(moved, over_z)
    table = [(s, s % n_row * n_col + s // n_row) for s in range(n_row * n_col)]
    return lead, permute_all(lead, table)


def spread_rows(rows, n_row, n_col):
    if (n_row, n_col) == (4, 8):
        spread_a, spread_b = block_tables(n_row, n_col)[2:4]
        return permute_all(rows, spread_a), permute_all(rows, spread_b)
    return (lax.all_gather(rows, "row", axis=0, tiled=True),)


def split_rows(pieces, n_row, n_col):
    if (n_row, n_col) == (4, 8):
        swap = block_tables(n_row, n_col)[4]
        pieces = [*pieces, *(permute_all(piece, swap) for piece in pieces)]
    split = []
    for piece in pieces:
        high = lax.reduce_precision(piece, 8, 7)
        split += [high.astype(jnp.bfloat16), (piece - high).astype(jnp.bfloat16)]
    return split


def product_kernel(count, place_ref, a_ref, *refs):
    side = pl.program_id(0)
    parts = place_ref.shape[0] - 1
    b_refs, out_refs = refs[: 2 * count * parts], refs[2 * count * parts :]
    deep = a_ref.shape[1] // parts
    sums = [None] * count
    for piece in range(parts):
        begin = pl.multiple_of(place_ref[1 + piece] * deep, deep) if parts > 1 else 0
        a = a_ref[:, pl.ds(begin, deep)]
        high = a.astype(jnp.bfloat16)
        low = (a - high.astype(jnp.float32)).astype(jnp.bfloat16)
        for i in range(count):
            spot = 2 * (i * parts + piece)
            b_high, b_low = b_refs[spot][...], b_refs[spot + 1][...]
            term = jnp.dot(high, b_high, preferred_element_type=jnp.float32)
            term += jnp.dot(high, b_low, preferred_element_type=jnp.float32)
            term += jnp.dot(low, b_high, preferred_element_type=jnp.float32)
            sums[i] = term if sums[i] is None else sums[i] + term

    @pl.when(side == 0)
    def _():
        for i in range(count):
            out_refs[2 * i][...] = sums[i]

    @pl.when(side == 1)
    def _():
        for i in range(count):
            out_refs[2 * i + 1][...] = sums[i]


def products(trailing, splits, place, n_col, step):
    rows, cols = trailing.shape
    half = rows // n_col // 2
    width = splits[0][0].shape[1]
    count, parts = len(splits), place.shape[0] - 1

    def a_index(side, place_ref):
        back = 1 + step
        spot = jnp.where(side == 0, place_ref[0] - back + n_col, place_ref[0] + back) % n_col
        return ring_column(n_col, spot) * 2 + side, 0

    spec = pltpu.PrefetchScalarGridSpec(
        num_scalar_prefetch=1,
        grid=(2,),
        in_specs=[pl.BlockSpec((half, cols), a_index)]
        + [pl.BlockSpec((cols // parts, width), lambda side, place_ref: (0, 0))]
        * (2 * count * parts),
        out_specs=[pl.BlockSpec((half, width), lambda side, place_ref: (0, 0))] * (2 * count),
    )
    sums = pl.pallas_call(
        functools.partial(product_kernel, count),
        grid_spec=spec,
        out_shape=[jax.ShapeDtypeStruct((half, width), jnp.float32)] * (2 * count),
        compiler_params=pltpu.CompilerParams(
            dimension_semantics=("arbitrary",), vmem_limit_bytes=VMEM
        ),
        cost_estimate=pl.CostEstimate(
            flops=2 * 3 * 2 * half * cols * width * count,
            bytes_accessed=4 * 2 * half * cols,
            transcendentals=0,
        ),
    )(place, trailing, *(part for split in splits for part in split))
    return [(sums[2 * i], sums[2 * i + 1]) for i in range(count)]


class Ring:
    def __init__(self, n_col):
        self.n_col, self.sent, self.step = n_col, (), 0

    def advance(self, made, *others):
        up, down = made
        if self.step:
            came_up = lax.ppermute(self.sent[0], "col", ring_perm(self.n_col, 1))
            came_down = lax.ppermute(self.sent[1], "col", ring_perm(self.n_col, -1))
            if others:
                came_up, came_down = after(came_up, *others), after(came_down, *others)
            up, down = came_up + up, came_down + down
        self.sent, self.step = (up, down), self.step + 1


def scatter_total(value, n, axes=("row", "col")):
    rows, cols = value.shape
    parts = lax.all_to_all(value.reshape(n, rows // n, cols), axes, 0, 0)
    return jnp.sum(parts, axis=0)


def spread_total(mine, n, axes=("row", "col")):
    spread = lax.all_to_all(jnp.broadcast_to(mine[None], (n,) + mine.shape), axes, 0, 0)
    return spread.reshape(-1, mine.shape[1])


def exchange_total(value):
    row_index = lax.axis_index("row")
    bits = [row_index % 2, row_index // 2]

    def partners(step):
        return [(i, i ^ step) for i in range(4)]

    for bit, step in zip(bits, (1, 2)):
        half = value.shape[0] // 2
        away = lax.dynamic_slice_in_dim(value, (1 - bit) * half, half, 0)
        kept = lax.dynamic_slice_in_dim(value, bit * half, half, 0)
        value = kept + lax.ppermute(away, "row", partners(step))
    value = spread_total(scatter_total(value, 8, "col"), 8, "col")
    for bit, step in ((bits[1], 2), (bits[0], 1)):
        other = lax.ppermute(value, "row", partners(step))
        value = jnp.where(
            bit == 0, jnp.concatenate([value, other], 0), jnp.concatenate([other, value], 0)
        )
    return value


def total(value, n_row, n_col):
    if (n_row, n_col) == (4, 8):
        return exchange_total(value)
    return spread_total(scatter_total(value, n_row * n_col), n_row * n_col)


def on_device(
    trailing, panel_first, panel_second, link_block, inverse_first, inverse_second, tile_struct
):
    n_row, n_col = lax.axis_size("row"), lax.axis_size("col")
    row_index, col_index = lax.axis_index("row"), lax.axis_index("col")
    count, width = panel_first.shape
    offset = (row_index * n_col + col_index) * count
    row_mask = jnp.repeat(tile_struct, TILE, axis=1)
    local_mask = lax.dynamic_slice_in_dim(row_mask, offset, count, 1).astype(jnp.float32)
    leads = (panel_first * local_mask[0][:, None], panel_second * local_mask[1][:, None])
    lead_first, lead_second = leads

    ring_place = jnp.where(col_index % 2 == 0, col_index // 2, n_col - (col_index + 1) // 2)
    if (n_row, n_col) == (4, 8):
        order = block_order(row_index, col_index)
    else:
        order = [0]
    place = jnp.stack([jnp.asarray(v, jnp.int32) for v in [ring_place] + order])

    moved, held_first = send_rows(lead_first, n_row, n_col)
    held_second = send_rows(lead_second, n_row, n_col, moved)[1]
    first, second = Ring(n_col), Ring(n_col)
    splits = [split_rows(spread_rows(held_first, n_row, n_col), n_row, n_col)]
    pieces = spread_rows(held_second, n_row, n_col)
    first.advance(products(trailing, splits, place, n_col, 0)[0])
    pieces = [after(piece, *first.sent) for piece in pieces]
    splits.append(split_rows(pieces, n_row, n_col))
    second.advance(products(trailing, splits[1:], after(place, *first.sent), n_col, 0)[0])
    for step in range(1, n_col):
        where = after(place, *first.sent, *second.sent)
        made = products(trailing, splits, where, n_col, step)
        first.advance(made[0])
        second.advance(made[1])
    panel_out_first = -jnp.concatenate(first.sent, 0)
    reach = jnp.concatenate(second.sent, 0)
    panel_out_second = -(matmul(panel_out_first, link_block) + reach)
    local = jnp.concatenate(
        [
            inner(lead_first, panel_out_first),
            inner(panel_out_first, lead_second),
            inner(lead_second, reach),
        ],
        1,
    )
    sums = total(local, n_row, n_col)
    diag_sum, cross_sum, reach_sum = (sums[:, i * width : (i + 1) * width] for i in range(3))
    diag_out_first = inverse_first - diag_sum
    cross_out_second = -(matmul(diag_out_first, link_block) + cross_sum)
    diag_out_second = (
        inverse_second
        - inner(link_block, cross_out_second)
        + matmul(cross_sum.T, link_block)
        + reach_sum
    )
    return (panel_out_first, diag_out_first, panel_out_second, cross_out_second, diag_out_second)


def solution(mesh):
    return jax.shard_map(
        on_device,
        mesh=mesh,
        in_specs=(
            P("row", "col"),
            P(("row", "col"), None),
            P(("row", "col"), None),
            P(),
            P(),
            P(),
            P(),
        ),
        out_specs=(P(("row", "col"), None), P(), P(("row", "col"), None), P(), P()),
        check_vma=False,
    )
```

```python
import functools

import jax
import jax.numpy as jnp
from jax import lax
from jax.experimental import pallas as pl
from jax.experimental.pallas import tpu as pltpu
from jax.sharding import PartitionSpec as P

TILE = 128
VMEM = 48 * 2**20


def matmul(left, right):
    return jnp.dot(left, right, precision=lax.Precision.HIGHEST, preferred_element_type=jnp.float32)


def inner(left, right):
    return lax.dot_general(
        left,
        right,
        (((0,), (0,)), ((), ())),
        precision=lax.Precision.HIGHEST,
        preferred_element_type=jnp.float32,
    )


def ring_column(n, place):
    return jnp.where(place < n // 2, 2 * place, 2 * (n - 1 - place) + 1)


def ring_perm(n, sign):
    order = list(range(0, n, 2)) + list(range(n - 1, 0, -2))
    return [(order[i], order[(i + sign) % n]) for i in range(n)]


def permute_all(value, table):
    return lax.ppermute(value, ("row", "col"), table)


def block_tables(n_row, n_col):
    def at(x, core, z, y):
        return (x * 2 + core) * n_col + z * 2 + y

    over_x, over_z, spread_a, spread_b, swap = [], [], [], [], []
    for x in range(2):
        for core in range(2):
            for z in range(4):
                for y in range(2):
                    here = at(x, core, z, y)
                    plane = (z + core) % 2
                    over_x.append((here, here if plane == x else at(1 - x, 1 - core, z, y)))
                    owner = x if (z + core) % 2 == x else 1 - x
                    own_core = core if owner == x else 1 - core
                    over_z.append((here, at(x, z // 2, 2 * owner + own_core, y)))
                    if core == y:
                        spread_a.append((here, at(1 - x, core, z, y)))
                        spread_b.append((here, here))
                    else:
                        spread_a.append((here, at(x, 1 - core, z, 1 - y)))
                        spread_b.append((here, at(1 - x, 1 - core, z, 1 - y)))
                    swap.append((here, at(x, 1 - core, z, y)))
    return over_x, over_z, spread_a, spread_b, swap


def block_order(row_index, col_index):
    x, core = row_index // 2, row_index % 2
    z, y = col_index // 2, col_index % 2
    even = (x + z) % 2
    order = []
    for who in (core, 1 - core):
        first = jnp.where(who == y, 1 - even, even)
        order += [first * 2 + who, (1 - first) * 2 + who]
    return order


def after(value, *others):
    return lax.optimization_barrier((value, others))[0]


def send_rows(lead, n_row, n_col, *ahead):
    if (n_row, n_col) == (4, 8):
        over_x, over_z = block_tables(n_row, n_col)[:2]
        moved = permute_all(after(lead, *ahead[:1]), over_x)
        return moved, permute_all(moved, over_z)
    table = [(s, s % n_row * n_col + s // n_row) for s in range(n_row * n_col)]
    return lead, permute_all(lead, table)


def spread_rows(rows, n_row, n_col):
    if (n_row, n_col) == (4, 8):
        spread_a, spread_b = block_tables(n_row, n_col)[2:4]
        return permute_all(rows, spread_a), permute_all(rows, spread_b)
    return (lax.all_gather(rows, "row", axis=0, tiled=True),)


def split_rows(pieces, n_row, n_col):
    if (n_row, n_col) == (4, 8):
        swap = block_tables(n_row, n_col)[4]
        pieces = [*pieces, *(permute_all(piece, swap) for piece in pieces)]
    split = []
    for piece in pieces:
        high = lax.reduce_precision(piece, 8, 7)
        split += [high.astype(jnp.bfloat16), (piece - high).astype(jnp.bfloat16)]
    return split


def product_kernel(count, place_ref, a_ref, *refs):
    side = pl.program_id(0)
    parts = place_ref.shape[0] - 1
    b_refs, out_refs = refs[: 2 * count * parts], refs[2 * count * parts :]
    deep = a_ref.shape[1] // parts
    sums = [None] * count
    for piece in range(parts):
        begin = pl.multiple_of(place_ref[1 + piece] * deep, deep) if parts > 1 else 0
        a = a_ref[:, pl.ds(begin, deep)]
        high = a.astype(jnp.bfloat16)
        low = (a - high.astype(jnp.float32)).astype(jnp.bfloat16)
        for i in range(count):
            spot = 2 * (i * parts + piece)
            b_high, b_low = b_refs[spot][...], b_refs[spot + 1][...]
            term = jnp.dot(high, b_high, preferred_element_type=jnp.float32)
            term += jnp.dot(high, b_low, preferred_element_type=jnp.float32)
            term += jnp.dot(low, b_high, preferred_element_type=jnp.float32)
            sums[i] = term if sums[i] is None else sums[i] + term

    @pl.when(side == 0)
    def _():
        for i in range(count):
            out_refs[2 * i][...] = sums[i]

    @pl.when(side == 1)
    def _():
        for i in range(count):
            out_refs[2 * i + 1][...] = sums[i]


def products(trailing, splits, place, n_col, step):
    rows, cols = trailing.shape
    half = rows // n_col // 2
    width = splits[0][0].shape[1]
    count, parts = len(splits), place.shape[0] - 1

    def a_index(side, place_ref):
        back = 1 + step
        spot = jnp.where(side == 0, place_ref[0] - back + n_col, place_ref[0] + back) % n_col
        return ring_column(n_col, spot) * 2 + side, 0

    spec = pltpu.PrefetchScalarGridSpec(
        num_scalar_prefetch=1,
        grid=(2,),
        in_specs=[pl.BlockSpec((half, cols), a_index)]
        + [pl.BlockSpec((cols // parts, width), lambda side, place_ref: (0, 0))]
        * (2 * count * parts),
        out_specs=[pl.BlockSpec((half, width), lambda side, place_ref: (0, 0))] * (2 * count),
    )
    sums = pl.pallas_call(
        functools.partial(product_kernel, count),
        grid_spec=spec,
        out_shape=[jax.ShapeDtypeStruct((half, width), jnp.float32)] * (2 * count),
        compiler_params=pltpu.CompilerParams(
            dimension_semantics=("arbitrary",), vmem_limit_bytes=VMEM
        ),
        cost_estimate=pl.CostEstimate(
            flops=2 * 3 * 2 * half * cols * width * count,
            bytes_accessed=4 * 2 * half * cols,
            transcendentals=0,
        ),
    )(place, trailing, *(part for split in splits for part in split))
    return [(sums[2 * i], sums[2 * i + 1]) for i in range(count)]


class Ring:
    def __init__(self, n_col):
        self.n_col, self.sent, self.step = n_col, (), 0

    def advance(self, made, *others):
        up, down = made
        if self.step:
            came_up = lax.ppermute(self.sent[0], "col", ring_perm(self.n_col, 1))
            came_down = lax.ppermute(self.sent[1], "col", ring_perm(self.n_col, -1))
            if others:
                came_up, came_down = after(came_up, *others), after(came_down, *others)
            up, down = came_up + up, came_down + down
        self.sent, self.step = (up, down), self.step + 1


def scatter_total(value, n, axes=("row", "col")):
    rows, cols = value.shape
    parts = lax.all_to_all(value.reshape(n, rows // n, cols), axes, 0, 0)
    return jnp.sum(parts, axis=0)


def spread_total(mine, n, axes=("row", "col")):
    spread = lax.all_to_all(jnp.broadcast_to(mine[None], (n,) + mine.shape), axes, 0, 0)
    return spread.reshape(-1, mine.shape[1])


def exchange_total(values, *others):
    row_index = lax.axis_index("row")
    bits = [row_index % 2, row_index // 2]

    def partners(step):
        return [(i, i ^ step) for i in range(4)]

    halved = []
    for value in values:
        for bit, step in zip(bits, (1, 2)):
            half = value.shape[0] // 2
            away = lax.dynamic_slice_in_dim(value, (1 - bit) * half, half, 0)
            kept = lax.dynamic_slice_in_dim(value, bit * half, half, 0)
            value = kept + lax.ppermute(away, "row", partners(step))
        halved.append(value)
    value = after(jnp.concatenate(halved, 1), *others)
    value = spread_total(scatter_total(value, 8, "col"), 8, "col")
    for bit, step in ((bits[1], 2), (bits[0], 1)):
        other = lax.ppermute(value, "row", partners(step))
        value = jnp.where(
            bit == 0, jnp.concatenate([value, other], 0), jnp.concatenate([other, value], 0)
        )
    return value


def total(values, n_row, n_col, *others):
    if (n_row, n_col) == (4, 8):
        return exchange_total(values, *others)
    mine = scatter_total(jnp.concatenate(values, 1), n_row * n_col)
    return spread_total(mine, n_row * n_col)


def on_device(
    trailing, panel_first, panel_second, link_block, inverse_first, inverse_second, tile_struct
):
    n_row, n_col = lax.axis_size("row"), lax.axis_size("col")
    row_index, col_index = lax.axis_index("row"), lax.axis_index("col")
    count, width = panel_first.shape
    offset = (row_index * n_col + col_index) * count
    row_mask = jnp.repeat(tile_struct, TILE, axis=1)
    local_mask = lax.dynamic_slice_in_dim(row_mask, offset, count, 1).astype(jnp.float32)
    leads = (panel_first * local_mask[0][:, None], panel_second * local_mask[1][:, None])
    lead_first, lead_second = leads

    ring_place = jnp.where(col_index % 2 == 0, col_index // 2, n_col - (col_index + 1) // 2)
    if (n_row, n_col) == (4, 8):
        order = block_order(row_index, col_index)
    else:
        order = [0]
    place = jnp.stack([jnp.asarray(v, jnp.int32) for v in [ring_place] + order])

    moved, held_first = send_rows(lead_first, n_row, n_col)
    held_second = send_rows(lead_second, n_row, n_col, moved)[1]
    first, second = Ring(n_col), Ring(n_col)
    splits = [split_rows(spread_rows(held_first, n_row, n_col), n_row, n_col)]
    pieces = spread_rows(held_second, n_row, n_col)
    first.advance(products(trailing, splits, place, n_col, 0)[0])
    begun = [value[:8, :TILE] for value in first.sent]
    pieces = [after(piece, *begun) for piece in pieces]
    splits.append(split_rows(pieces, n_row, n_col))
    second.advance(products(trailing, splits[1:], after(place, *first.sent), n_col, 0)[0])
    for step in range(1, n_col):
        where = after(place, *first.sent, *second.sent)
        made = products(trailing, splits, where, n_col, step)
        first.advance(made[0])
        second.advance(made[1])
    panel_out_first = -jnp.concatenate(first.sent, 0)
    reach = jnp.concatenate(second.sent, 0)
    panel_out_second = -(matmul(panel_out_first, link_block) + reach)
    both = jnp.concatenate(
        [inner(lead_first, panel_out_first), inner(panel_out_first, lead_second)], 1
    )
    sums = total([both, inner(lead_second, reach)], n_row, n_col, panel_out_second[:8, :TILE])
    diag_sum, cross_sum, reach_sum = (sums[:, i * width : (i + 1) * width] for i in range(3))
    diag_out_first = inverse_first - diag_sum
    cross_out_second = -(matmul(diag_out_first, link_block) + cross_sum)
    diag_out_second = (
        inverse_second
        - inner(link_block, cross_out_second)
        + matmul(cross_sum.T, link_block)
        + reach_sum
    )
    return (panel_out_first, diag_out_first, panel_out_second, cross_out_second, diag_out_second)


def solution(mesh):
    return jax.shard_map(
        on_device,
        mesh=mesh,
        in_specs=(
            P("row", "col"),
            P(("row", "col"), None),
            P(("row", "col"), None),
            P(),
            P(),
            P(),
            P(),
        ),
        out_specs=(P(("row", "col"), None), P(), P(("row", "col"), None), P(), P()),
        check_vma=False,
    )
```

```python
import functools

import jax
import jax.numpy as jnp
from jax import lax
from jax.experimental import pallas as pl
from jax.experimental.pallas import tpu as pltpu
from jax.sharding import PartitionSpec as P

TILE = 128
VMEM = 40 * 2**20


def matmul(left, right):
    return jnp.dot(left, right, precision=lax.Precision.HIGHEST, preferred_element_type=jnp.float32)


def inner(left, right):
    return lax.dot_general(
        left,
        right,
        (((0,), (0,)), ((), ())),
        precision=lax.Precision.HIGHEST,
        preferred_element_type=jnp.float32,
    )


def ring_column(n, place):
    return jnp.where(place < n // 2, 2 * place, 2 * (n - 1 - place) + 1)


def ring_perm(n, sign):
    order = list(range(0, n, 2)) + list(range(n - 1, 0, -2))
    return [(order[i], order[(i + sign) % n]) for i in range(n)]


def permute_all(value, table):
    return lax.ppermute(value, ("row", "col"), table)


def block_tables(n_row, n_col):
    def at(x, core, z, y):
        return (x * 2 + core) * n_col + z * 2 + y

    over_x, over_z, spread_a, spread_b, swap = [], [], [], [], []
    for x in range(2):
        for core in range(2):
            for z in range(4):
                for y in range(2):
                    here = at(x, core, z, y)
                    plane = (z + core) % 2
                    over_x.append((here, here if plane == x else at(1 - x, 1 - core, z, y)))
                    owner = x if (z + core) % 2 == x else 1 - x
                    own_core = core if owner == x else 1 - core
                    over_z.append((here, at(x, z // 2, 2 * owner + own_core, y)))
                    if core == y:
                        spread_a.append((here, at(1 - x, core, z, y)))
                        spread_b.append((here, here))
                    else:
                        spread_a.append((here, at(x, 1 - core, z, 1 - y)))
                        spread_b.append((here, at(1 - x, 1 - core, z, 1 - y)))
                    swap.append((here, at(x, 1 - core, z, y)))
    return over_x, over_z, spread_a, spread_b, swap


def block_order(row_index, col_index):
    x, core = row_index // 2, row_index % 2
    z, y = col_index // 2, col_index % 2
    even = (x + z) % 2
    order = []
    for who in (core, 1 - core):
        first = jnp.where(who == y, 1 - even, even)
        order += [first * 2 + who, (1 - first) * 2 + who]
    return order


def after(value, *others):
    return lax.optimization_barrier((value, others))[0]


def send_rows(lead, n_row, n_col, *ahead):
    if (n_row, n_col) == (4, 8):
        over_x, over_z = block_tables(n_row, n_col)[:2]
        moved = permute_all(after(lead, *ahead[:1]), over_x)
        return moved, permute_all(moved, over_z)
    table = [(s, s % n_row * n_col + s // n_row) for s in range(n_row * n_col)]
    return lead, permute_all(lead, table)


def spread_rows(rows, n_row, n_col):
    if (n_row, n_col) == (4, 8):
        spread_a, spread_b = block_tables(n_row, n_col)[2:4]
        return permute_all(rows, spread_a), permute_all(rows, spread_b)
    return (lax.all_gather(rows, "row", axis=0, tiled=True),)


def split_rows(pieces, n_row, n_col):
    if (n_row, n_col) == (4, 8):
        swap = block_tables(n_row, n_col)[4]
        pieces = [*pieces, *(permute_all(piece, swap) for piece in pieces)]
    split = []
    for piece in pieces:
        high = lax.reduce_precision(piece, 8, 7)
        split += [high.astype(jnp.bfloat16), (piece - high).astype(jnp.bfloat16)]
    return split


def product_kernel(count, place_ref, a_ref, *refs):
    side = pl.program_id(0)
    parts = place_ref.shape[0] - 1
    b_refs, out_refs = refs[: 2 * count * parts], refs[2 * count * parts :]
    deep = a_ref.shape[1] // parts
    sums = [None] * count
    for piece in range(parts):
        begin = pl.multiple_of(place_ref[1 + piece] * deep, deep) if parts > 1 else 0
        a = a_ref[:, pl.ds(begin, deep)]
        high = a.astype(jnp.bfloat16)
        low = (a - high.astype(jnp.float32)).astype(jnp.bfloat16)
        for i in range(count):
            spot = 2 * (i * parts + piece)
            b_high, b_low = b_refs[spot][...], b_refs[spot + 1][...]
            term = jnp.dot(high, b_high, preferred_element_type=jnp.float32)
            term += jnp.dot(high, b_low, preferred_element_type=jnp.float32)
            term += jnp.dot(low, b_high, preferred_element_type=jnp.float32)
            sums[i] = term if sums[i] is None else sums[i] + term

    @pl.when(side == 0)
    def _():
        for i in range(count):
            out_refs[2 * i][...] = sums[i]

    @pl.when(side == 1)
    def _():
        for i in range(count):
            out_refs[2 * i + 1][...] = sums[i]


def products(trailing, splits, place, n_col, step):
    rows, cols = trailing.shape
    half = rows // n_col // 2
    width = splits[0][0].shape[1]
    count, parts = len(splits), place.shape[0] - 1

    def a_index(side, place_ref):
        back = 1 + step
        spot = jnp.where(side == 0, place_ref[0] - back + n_col, place_ref[0] + back) % n_col
        return ring_column(n_col, spot) * 2 + side, 0

    spec = pltpu.PrefetchScalarGridSpec(
        num_scalar_prefetch=1,
        grid=(2,),
        in_specs=[pl.BlockSpec((half, cols), a_index)]
        + [pl.BlockSpec((cols // parts, width), lambda side, place_ref: (0, 0))]
        * (2 * count * parts),
        out_specs=[pl.BlockSpec((half, width), lambda side, place_ref: (0, 0))] * (2 * count),
    )
    sums = pl.pallas_call(
        functools.partial(product_kernel, count),
        grid_spec=spec,
        out_shape=[jax.ShapeDtypeStruct((half, width), jnp.float32)] * (2 * count),
        compiler_params=pltpu.CompilerParams(
            dimension_semantics=("arbitrary",), vmem_limit_bytes=VMEM
        ),
        cost_estimate=pl.CostEstimate(
            flops=2 * 3 * 2 * half * cols * width * count,
            bytes_accessed=4 * 2 * half * cols,
            transcendentals=0,
        ),
    )(place, trailing, *(part for split in splits for part in split))
    return [(sums[2 * i], sums[2 * i + 1]) for i in range(count)]


class Ring:
    def __init__(self, n_col):
        self.n_col, self.sent, self.step = n_col, (), 0

    def advance(self, made, *others):
        up, down = made
        if self.step:
            came_up = lax.ppermute(self.sent[0], "col", ring_perm(self.n_col, 1))
            came_down = lax.ppermute(self.sent[1], "col", ring_perm(self.n_col, -1))
            if others:
                came_up, came_down = after(came_up, *others), after(came_down, *others)
            up, down = came_up + up, came_down + down
        self.sent, self.step = (up, down), self.step + 1


def scatter_total(value, n, axes=("row", "col")):
    rows, cols = value.shape
    parts = lax.all_to_all(value.reshape(n, rows // n, cols), axes, 0, 0)
    return jnp.sum(parts, axis=0)


def spread_total(mine, n, axes=("row", "col")):
    spread = lax.all_to_all(jnp.broadcast_to(mine[None], (n,) + mine.shape), axes, 0, 0)
    return spread.reshape(-1, mine.shape[1])


def exchange_total(values, *others):
    row_index = lax.axis_index("row")
    bits = [row_index % 2, row_index // 2]

    def partners(step):
        return [(i, i ^ step) for i in range(4)]

    halved = []
    for value in values:
        for bit, step in zip(bits, (1, 2)):
            half = value.shape[0] // 2
            away = lax.dynamic_slice_in_dim(value, (1 - bit) * half, half, 0)
            kept = lax.dynamic_slice_in_dim(value, bit * half, half, 0)
            value = kept + lax.ppermute(away, "row", partners(step))
        halved.append(value)
    value = after(jnp.concatenate(halved, 1), *others)
    value = spread_total(scatter_total(value, 8, "col"), 8, "col")
    for bit, step in ((bits[1], 2), (bits[0], 1)):
        other = lax.ppermute(value, "row", partners(step))
        value = jnp.where(
            bit == 0, jnp.concatenate([value, other], 0), jnp.concatenate([other, value], 0)
        )
    return value


def total(values, n_row, n_col, *others):
    if (n_row, n_col) == (4, 8):
        return exchange_total(values, *others)
    mine = scatter_total(jnp.concatenate(values, 1), n_row * n_col)
    return spread_total(mine, n_row * n_col)


def on_device(
    trailing, panel_first, panel_second, link_block, inverse_first, inverse_second, tile_struct
):
    n_row, n_col = lax.axis_size("row"), lax.axis_size("col")
    row_index, col_index = lax.axis_index("row"), lax.axis_index("col")
    count, width = panel_first.shape
    offset = (row_index * n_col + col_index) * count
    row_mask = jnp.repeat(tile_struct, TILE, axis=1)
    local_mask = lax.dynamic_slice_in_dim(row_mask, offset, count, 1).astype(jnp.float32)
    leads = (panel_first * local_mask[0][:, None], panel_second * local_mask[1][:, None])
    lead_first, lead_second = leads

    ring_place = jnp.where(col_index % 2 == 0, col_index // 2, n_col - (col_index + 1) // 2)
    if (n_row, n_col) == (4, 8):
        order = block_order(row_index, col_index)
    else:
        order = [0]
    place = jnp.stack([jnp.asarray(v, jnp.int32) for v in [ring_place] + order])

    moved, held_first = send_rows(lead_first, n_row, n_col)
    held_second = send_rows(lead_second, n_row, n_col, moved)[1]
    first, second = Ring(n_col), Ring(n_col)
    splits = [split_rows(spread_rows(held_first, n_row, n_col), n_row, n_col)]
    pieces = spread_rows(held_second, n_row, n_col)
    first.advance(products(trailing, splits, place, n_col, 0)[0])
    begun = [value[:8, :TILE] for value in first.sent]
    pieces = [after(piece, *begun) for piece in pieces]
    splits.append(split_rows(pieces, n_row, n_col))
    second.advance(products(trailing, splits[1:], after(place, *first.sent), n_col, 0)[0])
    for step in range(1, n_col):
        where = after(place, *first.sent, *second.sent)
        made = products(trailing, splits, where, n_col, step)
        first.advance(made[0])
        second.advance(made[1])
    panel_out_first = -jnp.concatenate(first.sent, 0)
    reach = jnp.concatenate(second.sent, 0)
    panel_out_second = -(matmul(panel_out_first, link_block) + reach)
    both = jnp.concatenate(
        [inner(lead_first, panel_out_first), inner(panel_out_first, lead_second)], 1
    )
    sums = total([both, inner(lead_second, reach)], n_row, n_col, panel_out_second[:8, :TILE])
    diag_sum, cross_sum, reach_sum = (sums[:, i * width : (i + 1) * width] for i in range(3))
    diag_out_first = inverse_first - diag_sum
    cross_out_second = -(matmul(diag_out_first, link_block) + cross_sum)
    diag_out_second = (
        inverse_second
        - inner(link_block, cross_out_second)
        + matmul(cross_sum.T, link_block)
        + reach_sum
    )
    return (panel_out_first, diag_out_first, panel_out_second, cross_out_second, diag_out_second)


def solution(mesh):
    return jax.shard_map(
        on_device,
        mesh=mesh,
        in_specs=(
            P("row", "col"),
            P(("row", "col"), None),
            P(("row", "col"), None),
            P(),
            P(),
            P(),
            P(),
        ),
        out_specs=(P(("row", "col"), None), P(), P(("row", "col"), None), P(), P()),
        check_vma=False,
    )
```
